32 devices in a mesh: grp: 4 (over z), mem: 8 (over y, x, core).
Axes of the slice: x: 2, y: 2, z: 4, core: 2. Of those that a mesh axis runs over, the one named last changes fastest.
Arguments:
- embeddings: bfloat16 [12288, 1024], P(('grp', 'mem')), may hold values from -6 to 6
- row_target: int32 [12288, 1], P(('grp', 'mem')), may hold values from 0 to 31; in each aligned block of 384 rows (0 to 383, 384 to 767, ...) at most 24 rows name the same one
Outputs:
- best_cosine: float32 [12288], P(('grp', 'mem'))
The draws below stay inside these ranges and needn't reach their ends.
Inputs may be any that keep to these rules, and one draw needn't show every extreme that they name: `row_target`: among the rows of one device no owner device is named by more than 24 rows, a bound that some block reaches.
All inputs are finite; a program needn't handle non-finite values.
Results may differ from the reference program's by a relative error of at most 0.0012.
Values may be sent and summed in bfloat16 or wider, within the bound.
A program may use at most 128 MiB of HBM per device.

```python
import math
import jax
import jax.numpy as jnp
import numpy as np
from jax import lax

D = 1024
ROW_DEV = 384
CAP = 24
SLOTS = 768
ROWS = 12288
N_GRP = 4
N_MEM = 8
DEVICES = 32


def block_scale(rng, extent, pieces, smallest, top_value):
    factor_of = 1.0
    for dim, shards_of in pieces:
        heights = jax.random.uniform(jax.random.fold_in(jax.random.fold_in(rng, 6), dim), (shards_of,), jnp.float32, smallest / len(pieces), top_value / len(pieces))
        factor_of = factor_of * jnp.repeat(jnp.exp(heights), extent[dim] // shards_of).reshape((-1,) + (1,) * (len(extent) - 1 - dim))
    return factor_of


def deal_out(stream_key, own, number, rows, amount, top, bound, lean):
    order = jax.random.permutation(stream_key, amount)
    packed, usual = load_shares(amount, rows * top, bound, lean, True), load_shares(amount, rows * top, bound, lean, False)
    places = jnp.arange(amount)

    def named(tallies, offset_by):
        used = int((tallies > 0).sum())
        fixed = max(1, used // 4)
        moved = fixed + (places - fixed + offset_by * (used - fixed)) % max(1, amount - fixed)
        return jnp.zeros((amount,), jnp.int32).at[order[jnp.where(places < fixed, places, moved)]].set(jnp.asarray(tallies, jnp.int32))

    tallies = jnp.where(number % 4 == 0, named(packed, number // 4), named(usual, number - number // 4 - 1))
    mixed = jax.random.permutation(jax.random.fold_in(own, 3), amount)
    giver, receiver = mixed[0:amount // 2 * 2:2], mixed[1:amount // 2 * 2:2]
    room = jnp.minimum(tallies[giver] - 1, bound - tallies[receiver]) // 2
    room = jnp.where((giver == order[0]) | (receiver == order[0]) | (tallies[receiver] == 0), 0, jnp.maximum(room, 0))
    moved = jax.random.randint(jax.random.fold_in(own, 4), (amount // 2,), 0, 1 << 20) % (room + 1)
    tallies = tallies.at[giver].add(-moved).at[receiver].add(moved)
    labels = jnp.searchsorted(jnp.cumsum(tallies), jnp.arange(rows * top), side="right").astype(jnp.int32)
    table = labels.reshape(top, rows).T
    table = table[jax.random.permutation(jax.random.fold_in(own, 1), rows)]
    offset_by = jax.random.randint(jax.random.fold_in(own, 2), (rows, 1), 0, top)
    return jnp.take_along_axis(table, (jnp.arange(top)[None, :] + offset_by) % top, axis=1)


def load_shares(number_of, total, bound, skew, full):
    portions = [(1 << 20) // math.isqrt(grade ** skew) + 1 for grade in range(1, number_of + 1)]
    largest = bound if full else min(bound, max(-(-total // number_of), total * portions[0] // sum(portions)))
    least = 1 if total - largest >= number_of - 1 else 0
    holding, rest = [largest] + [least] * (number_of - 1), total - largest - least * (number_of - 1)
    while rest > 0:
        movable = [i for i in range(1, number_of) if holding[i] < largest] or [i for i in range(1, number_of) if holding[i] < bound]
        whole, left = sum([portions[i] for i in movable]), rest
        for i in movable:
            addition = min(bound - holding[i], max(1, left * portions[i] // whole), rest)
            holding[i] = holding[i] + addition
            rest = rest - addition
    return np.array(holding)


def normal_values(stream_key, dims, scale, limit, split=(), kind=jnp.bfloat16):
    values = jax.random.normal(stream_key, dims, jnp.float32) * scale
    if len(split) > 0:
        values = block_scale(stream_key, dims, split, -0.22, 0.18) * values
    return jnp.clip(values, min=-limit, max=limit).astype(kind)


def setup_inputs(seed: int = 0) -> dict:
    keys = jax.random.split(jax.random.key(seed), 3)
    embeddings = normal_values(keys[0], (ROWS, D), 1.0, 6.0, ((0, 32),))
    row_target_keys = jax.random.split(jax.random.fold_in(keys[1], 1), ROWS // ROW_DEV)
    row_target_turns = jax.random.permutation(jax.random.fold_in(keys[1], 3), ROWS // ROW_DEV)
    row_target = jax.vmap(lambda own, number: deal_out(jax.random.fold_in(keys[1], 2), own, number, ROW_DEV, DEVICES, 1, CAP, 2))(row_target_keys, row_target_turns).reshape((ROWS, 1))
    return dict(embeddings=embeddings, row_target=row_target)


def reference(embeddings, row_target):
    values = embeddings.astype(jnp.float32)
    inv_norm = lax.rsqrt(lax.optimization_barrier(jnp.mean(values * values, axis=1, keepdims=True)) + 1e-06) * (1.0 / math.sqrt(D))
    unit_rows = (values * inv_norm).astype(jnp.bfloat16)
    target = row_target[:, 0].reshape(DEVICES, ROW_DEV)
    onehot = (target[:, :, None] == jnp.arange(DEVICES, dtype=jnp.int32)[None, None, :]).astype(jnp.int32)
    running = jnp.cumsum(onehot, axis=1)
    slot_index = lax.optimization_barrier(jnp.sum(onehot * running, axis=2)) - 1
    source = jnp.arange(DEVICES, dtype=jnp.int32)[:, None]
    position = (source * CAP + slot_index).reshape(-1).astype(jnp.int32)
    owner_dev = target.reshape(-1).astype(jnp.int32)
    held_rows = jnp.zeros((DEVICES, SLOTS, D), jnp.bfloat16).at[owner_dev, position].set(unit_rows)
    held_ident = jnp.full((DEVICES, SLOTS), ROWS, jnp.int32).at[owner_dev, position].set(jnp.arange(ROWS, dtype=jnp.int32))
    grouped = held_rows.reshape(N_GRP, N_MEM * SLOTS, D)
    grouped_ident = held_ident.reshape(N_GRP, N_MEM * SLOTS)

    def per_device(device):
        own_block = held_rows[device]
        row_ident = held_ident[device]
        group_index = device // N_MEM
        others = grouped[group_index]
        other_ident = grouped_ident[group_index]
        cosines = lax.dot_general(own_block, others, (((1,), (1,)), ((), ())), preferred_element_type=jnp.float32)
        keep_mask = (other_ident[None, :] < ROWS) & (other_ident[None, :] != row_ident[:, None])
        return jnp.maximum(lax.optimization_barrier(jnp.max(jnp.where(keep_mask, cosines, -1.0), axis=1)), -1.0)
    best_value = lax.map(per_device, jnp.arange(DEVICES, dtype=jnp.int32))
    return jnp.zeros((ROWS,), jnp.float32).at[held_ident.reshape(-1)].set(best_value.reshape(-1), mode='drop')
```

```python
import functools
import math

import jax
import jax.numpy as jnp
from jax import lax
from jax.experimental import pallas as pl
from jax.experimental.pallas import tpu as pltpu
from jax.sharding import PartitionSpec as P

MESH = pl.DeviceIdType.MESH
LANES = 128
TAG = 16


def kernel(
    groups, members, emb_ref, target_ref, out_ref,
    plane, line, seen, plane_out, line_out, plane_in, line_in, own_best, line_best,
    ring_send, ring_recv, pass_send, line_send, line_recv,
    back_send, back_recv, home_send, home_recv,
):
    rows, width = emb_ref.shape
    half = members // 2
    g, m = lax.axis_index("grp"), lax.axis_index("mem")
    full = (groups - 1) // 2
    has_half = groups % 2 == 0
    steps = list(range(1, full + 1)) + ([groups // 2] if has_half else [])
    lines = len(steps)

    def partner_of(i):
        return i + 1 - 2 * lax.rem(i, 2)

    if has_half:
        low = lax.rem(g, groups // 2)
        upper = g // (groups // 2)
        takes_half = lax.rem(low + upper, 2) == 1
        gives_half = lax.rem(low + upper, 2) == 0

    def if_takes(j, body):
        if j < full:
            body()
        else:
            pl.when(takes_half)(body)

    def if_gives(j, body):
        if j < full:
            body()
        else:
            pl.when(gives_half)(body)

    barrier = pltpu.get_barrier_semaphore()
    for i in range(1, members):
        pl.semaphore_signal(
            barrier, inc=1, device_id=(g, lax.rem(m + i, members)), device_id_type=MESH
        )
    for i in range(1, groups):
        pl.semaphore_signal(
            barrier, inc=1, device_id=(lax.rem(g + i, groups), m), device_id_type=MESH
        )

    values = emb_ref[...].astype(jnp.float32)
    inv_norm = lax.rsqrt(jnp.mean(values * values, axis=1, keepdims=True) + 1e-06) * (
        1.0 / math.sqrt(width)
    )
    plane[0, pl.ds(0, rows), :] = (values * inv_norm).astype(jnp.bfloat16)
    cluster = jnp.floor((target_ref[...].astype(jnp.float32) + 0.5) * (1.0 / members))
    plane[0, pl.ds(rows, TAG), :] = jnp.zeros((TAG, width), jnp.bfloat16)
    plane[0, pl.ds(rows, TAG), pl.ds(0, rows)] = jnp.broadcast_to(cluster, (TAG, rows)).astype(
        jnp.bfloat16
    )

    pl.semaphore_wait(barrier, members - 1 + groups - 1)

    def line_copy(j):
        return pltpu.make_async_remote_copy(
            src_ref=plane.at[0], dst_ref=line.at[j],
            send_sem=line_send.at[j], recv_sem=line_recv.at[j],
            device_id=(lax.rem(g + groups - steps[j], groups), m), device_id_type=MESH,
        )

    def ring_copy(s):
        return pltpu.make_async_remote_copy(
            src_ref=plane.at[0], dst_ref=plane.at[2 * s],
            send_sem=ring_send.at[s], recv_sem=ring_recv.at[2 * s],
            device_id=(g, lax.rem(m + members - 2 * s, members)), device_id_type=MESH,
        )

    def pass_copy(s):
        return pltpu.make_async_remote_copy(
            src_ref=plane.at[2 * s], dst_ref=plane.at[2 * s + 1],
            send_sem=pass_send.at[s], recv_sem=ring_recv.at[2 * s + 1],
            device_id=(g, partner_of(m)), device_id_type=MESH,
        )

    for j in range(lines):
        if_gives(j, lambda j=j: line_copy(j).start())
    for s in range(1, half):
        ring_copy(s).start()
    pass_copy(0).start()

    def cluster_row(ref, i):
        return ref[i, pl.ds(rows, TAG), pl.ds(0, rows)].astype(jnp.float32)[0:1, :]

    def cluster_columns(i):
        seen[...] = jnp.transpose(jnp.broadcast_to(cluster_row(plane, i), (LANES, rows)))

    def cosines(i, left):
        return lax.dot_general(
            plane[i, pl.ds(0, rows), :], left, (((1,), (1,)), ((), ())),
            preferred_element_type=jnp.float32,
        )

    def masked(cos, across, k, same):
        part = cos[:, k * LANES:(k + 1) * LANES]
        keep = seen[...] == across[:, k * LANES:(k + 1) * LANES]
        if same:
            down = lax.broadcasted_iota(jnp.int32, (rows, LANES), 0)
            over = lax.broadcasted_iota(jnp.int32, (rows, LANES), 1) + k * LANES
            keep = keep & (down != over)
        return jnp.where(keep, part, -1.0)

    own_best[...] = jnp.full((8, rows), -1.0, jnp.float32)
    line_best[...] = jnp.full((lines, 8, rows), -1.0, jnp.float32)

    def own_pairs(i, same=False):
        cluster_columns(i)
        cos = cosines(i, plane[0, pl.ds(0, rows), :])
        across = cluster_row(plane, 0)
        for k in range(rows // LANES):
            at = pl.ds(k * LANES, LANES)
            best = jnp.max(masked(cos, across, k, same), axis=0, keepdims=True)
            own_best[:, at] = jnp.maximum(own_best[:, at], best)

    own_pairs(0, True)

    def even(s, carry):
        ring_copy(s).wait_recv()
        pass_copy(s).start()
        own_pairs(2 * s)
        return carry

    def odd(s, carry):
        pass_copy(s).wait_recv()
        own_pairs(2 * s + 1)
        return carry

    lax.fori_loop(1, half, even, 0)
    lax.fori_loop(0, half, odd, 0)

    for j in range(lines):
        if_takes(j, lambda j=j: line_copy(j).wait_recv())

    def line_pairs(j, i, reached):
        cos = cosines(i, line[j, pl.ds(0, rows), :])
        across = cluster_row(line, j)
        for k in range(rows // LANES):
            at = pl.ds(k * LANES, LANES)
            part = masked(cos, across, k, False)
            line_best[j, :, at] = jnp.maximum(
                line_best[j, :, at], jnp.max(part, axis=0, keepdims=True)
            )
            reached[...] = jnp.maximum(reached[...], part)

    def back_copy(i):
        above = lax.rem(m + 2 * (i // 2), members)
        holder = lax.rem(i, 2) * partner_of(above) + (1 - lax.rem(i, 2)) * above
        return pltpu.make_async_remote_copy(
            src_ref=plane_out.at[i], dst_ref=plane_in.at[i],
            send_sem=back_send.at[i], recv_sem=back_recv.at[i],
            device_id=(g, holder), device_id_type=MESH,
        )

    def home_copy(j):
        return pltpu.make_async_remote_copy(
            src_ref=line_out.at[j], dst_ref=line_in.at[j],
            send_sem=home_send.at[j], recv_sem=home_recv.at[j],
            device_id=(lax.rem(g + steps[j], groups), m), device_id_type=MESH,
        )

    def across_lines(i, reached):
        cluster_columns(i)
        reached[...] = jnp.full((rows, LANES), -1.0, jnp.float32)
        for j in range(lines):
            if_takes(j, lambda j=j: line_pairs(j, i, reached))
        best = jnp.max(jnp.transpose(reached[...]), axis=0, keepdims=True)
        plane_out[i] = jnp.broadcast_to(best, (8, rows))

    def with_reached(reached):
        def step(i, carry):
            across_lines(i, reached)
            back_copy(i).start()
            return carry

        lax.fori_loop(1, members, step, 0)
        across_lines(0, reached)

    pl.run_scoped(with_reached, pltpu.VMEM((rows, LANES), jnp.float32))

    def send_home(j):
        line_out[j] = line_best[j]
        home_copy(j).start()

    for j in range(lines):
        if_takes(j, lambda j=j: send_home(j))

    own_best[...] = jnp.maximum(own_best[...], plane_out[0])

    def collect(i, carry):
        back_copy(i).wait_recv()
        own_best[...] = jnp.maximum(own_best[...], plane_in[i])
        return carry

    lax.fori_loop(1, members, collect, 0)

    def collect_home(j):
        home_copy(j).wait_recv()
        own_best[...] = jnp.maximum(own_best[...], line_in[j])

    for j in range(lines):
        if_gives(j, lambda j=j: collect_home(j))
    out_ref[...] = own_best[0:1, :]

    for j in range(lines):
        if_gives(j, lambda j=j: line_copy(j).wait_send())
        if_takes(j, lambda j=j: home_copy(j).wait_send())
    for s in range(half):
        if s > 0:
            ring_copy(s).wait_send()
        pass_copy(s).wait_send()
    for i in range(1, members):
        back_copy(i).wait_send()


def per_device(embeddings, row_target):
    rows, width = embeddings.shape
    groups = lax.axis_size("grp")
    members = lax.axis_size("mem")
    lines = groups // 2
    block = (rows + TAG, width)
    dma = pltpu.SemaphoreType.DMA
    f32 = jnp.float32
    best = pl.pallas_call(
        functools.partial(kernel, groups, members),
        out_shape=jax.ShapeDtypeStruct((1, rows), f32),
        in_specs=[pl.BlockSpec(memory_space=pltpu.VMEM)] * 2,
        out_specs=pl.BlockSpec(memory_space=pltpu.VMEM),
        scratch_shapes=[
            pltpu.VMEM((members, *block), jnp.bfloat16),
            pltpu.VMEM((lines, *block), jnp.bfloat16),
            pltpu.VMEM((rows, LANES), f32),
            pltpu.VMEM((members, 8, rows), f32),
            pltpu.VMEM((lines, 8, rows), f32),
            pltpu.VMEM((members, 8, rows), f32),
            pltpu.VMEM((lines, 8, rows), f32),
            pltpu.VMEM((8, rows), f32),
            pltpu.VMEM((lines, 8, rows), f32),
            dma((members // 2,)),
            dma((members,)),
            dma((members // 2,)),
            dma((lines,)),
            dma((lines,)),
            dma((members,)),
            dma((members,)),
            dma((lines,)),
            dma((lines,)),
        ],
        compiler_params=pltpu.CompilerParams(
            collective_id=0, has_side_effects=True, vmem_limit_bytes=48 * 2**20
        ),
    )(embeddings, row_target.reshape(1, rows))
    return best.reshape(rows)


def solution(mesh):
    in_specs = (P(("grp", "mem"), None), P(("grp", "mem"), None))
    return jax.shard_map(
        per_device, mesh=mesh, in_specs=in_specs, out_specs=P(("grp", "mem")), check_vma=False
    )
```

```python
import functools
import math

import jax
import jax.numpy as jnp
from jax import lax
from jax.experimental import pallas as pl
from jax.experimental.pallas import tpu as pltpu
from jax.sharding import PartitionSpec as P

MESH = pl.DeviceIdType.MESH
LANES = 128
SUBLANES = 8


def xor(a, b, count):
    total, bit = 0, 1
    while bit < count:
        one, other = lax.rem(a // bit, 2), (b // bit) % 2
        total = total + bit * (one + other - 2 * one * other)
        bit *= 2
    return total


def kernel(
    groups, members, emb_ref, target_ref, out_ref,
    plane, line, plane_tag, line_tag, seen, reached, plane_out, line_out, plane_in, line_in, own_best,
    ring_send, ring_recv, line_send, line_recv,
    tag_send, tag_recv, end_send, end_recv,
    back_send, back_recv, home_send, home_recv,
):
    rows, width = emb_ref.shape
    pieces = rows // LANES
    g, m = lax.axis_index("grp"), lax.axis_index("mem")
    full = (groups - 1) // 2
    has_half = groups % 2 == 0
    steps = list(range(1, full + 1)) + ([groups // 2] if has_half else [])
    lines = len(steps)
    halves = [pl.ds(0, rows // 2), pl.ds(rows // 2, rows // 2)]
    parts = [(0, pieces - 1), (pieces - 1, pieces)]
    relayed = members == 8

    if has_half:
        low = lax.rem(g, groups // 2)
        upper = g // (groups // 2)
        takes_half = lax.rem(low + upper, 2) == 1
        gives_half = lax.rem(low + upper, 2) == 0

    def if_takes(j, body):
        if j < full:
            body()
        else:
            pl.when(takes_half)(body)

    def if_gives(j, body):
        if j < full:
            body()
        else:
            pl.when(gives_half)(body)

    def member(i):
        return (g, xor(m, i, members))

    def group_below(j):
        return (lax.rem(g + groups - steps[j], groups), m)

    barrier = pltpu.get_barrier_semaphore()
    for i in range(1, members):
        pl.semaphore_signal(barrier, inc=1, device_id=member(i), device_id_type=MESH)
    for i in range(1, groups):
        pl.semaphore_signal(
            barrier, inc=1, device_id=(lax.rem(g + i, groups), m), device_id_type=MESH
        )

    values = emb_ref[...].astype(jnp.float32)
    inv_norm = lax.rsqrt(jnp.mean(values * values, axis=1, keepdims=True) + 1e-06) * (
        1.0 / math.sqrt(width)
    )
    plane[0] = (values * inv_norm).astype(jnp.bfloat16)
    cluster = jnp.floor((target_ref[...].astype(jnp.float32) + 0.5) * (1.0 / members))
    plane_tag[0] = jnp.zeros((SUBLANES, LANES), jnp.float32)
    for k in range(pieces):
        plane_tag[0, k:k + 1, :] = cluster[:, k * LANES:(k + 1) * LANES]

    pl.semaphore_wait(barrier, members - 1 + groups - 1)

    def line_copy(j, p):
        at = pl.ds(parts[p][0] * LANES, (parts[p][1] - parts[p][0]) * LANES)
        return pltpu.make_async_remote_copy(
            src_ref=plane.at[0, at], dst_ref=line.at[j, at],
            send_sem=line_send.at[j, p], recv_sem=line_recv.at[j, p],
            device_id=group_below(j), device_id_type=MESH,
        )

    def plane_copy(held, to, h):
        slot = held ^ to
        return pltpu.make_async_remote_copy(
            src_ref=plane.at[held, halves[h]], dst_ref=plane.at[slot, halves[h]],
            send_sem=ring_send.at[slot, h], recv_sem=ring_recv.at[slot, h],
            device_id=member(to), device_id_type=MESH,
        )

    def tag_copy(i):
        return pltpu.make_async_remote_copy(
            src_ref=plane_tag.at[0], dst_ref=plane_tag.at[i],
            send_sem=tag_send.at[i], recv_sem=tag_recv.at[i],
            device_id=member(i), device_id_type=MESH,
        )

    def end_copy(j):
        return pltpu.make_async_remote_copy(
            src_ref=plane_tag.at[0], dst_ref=line_tag.at[j],
            send_sem=end_send.at[j], recv_sem=end_recv.at[j],
            device_id=group_below(j), device_id_type=MESH,
        )

    plan = {}
    for slot in range(2, members, 2):
        for h in range(2):
            plan[slot, h] = (0, slot)
    if relayed:
        order = [(2, 0), (4, 1), (2, 1), (4, 0), (6, 0), (6, 1)]
        plan[6, 0], plan[6, 1] = (2, 4), (4, 2)
    else:
        order = [(slot, h) for slot in range(2, members, 2) for h in range(2)]

    for i in range(1, members):
        tag_copy(i).start()
    for j in range(lines):
        if_gives(j, lambda j=j: end_copy(j).start())
    first = [key for key in order if plan[key][0] == 0]
    for p in range(2):
        for h, to in [(h, to) for to, h in first[p * len(first) // 2:(p + 1) * len(first) // 2]]:
            plane_copy(0, to, h).start()
        for j in range(lines):
            if_gives(j, lambda j=j, p=p: line_copy(j, p).start())
    for h in range(2):
        plane_copy(0, 1, h).start()

    def see(i):
        for k in range(pieces):
            row = jnp.broadcast_to(plane_tag[i, k:k + 1, :], (LANES, LANES))
            seen[k * LANES:(k + 1) * LANES, :] = jnp.transpose(row)

    def cosines(i, left):
        return lax.dot_general(
            plane[i], left, (((1,), (1,)), ((), ())), preferred_element_type=jnp.float32
        )

    own_best[...] = jnp.full((SUBLANES, rows), -1.0, jnp.float32)
    line_out[...] = jnp.full((lines, SUBLANES, rows), -1.0, jnp.float32)
    plane_out[...] = jnp.full((members, SUBLANES, rows), -1.0, jnp.float32)

    def own_pairs(i, same=False):
        see(i)
        cos = cosines(i, plane[0])
        for k in range(pieces):
            at = pl.ds(k * LANES, LANES)
            keep = seen[...] == plane_tag[0, k:k + 1, :]
            if same:
                down = lax.broadcasted_iota(jnp.int32, (rows, LANES), 0)
                over = lax.broadcasted_iota(jnp.int32, (rows, LANES), 1) + k * LANES
                keep = keep & (down != over)
            part = jnp.where(keep, cos[:, k * LANES:(k + 1) * LANES], -1.0)
            own_best[:, at] = jnp.maximum(own_best[:, at], jnp.max(part, axis=0, keepdims=True))

    own_pairs(0, True)
    for i in range(1, members):
        tag_copy(i).wait_recv()
    for j in range(lines):
        if_takes(j, lambda j=j: end_copy(j).wait_recv())

    def arrive(slot, h):
        held, to = plan[slot, h]
        plane_copy(held, to, h).wait_recv()
        for key, (source, onto) in plan.items():
            if source == slot and key[1] == h:
                plane_copy(source, onto, h).start()
        plane_copy(slot, 1, h).start()

    for h in range(2):
        plane_copy(0, 1, h).wait_recv()
    own_pairs(1)
    have = 0
    for slot, h in order:
        arrive(slot, h)
        if slot == 4 and h == 0 and relayed:
            for i in (2, 4):
                own_pairs(i)
            have = 4
    for i in range(2, members):
        if i % 2:
            for h in range(2):
                plane_copy(i - 1, 1, h).wait_recv()
        if not (have and i in (2, 4)):
            own_pairs(i)

    def line_pairs(j, i, p):
        start, stop = parts[p]
        cos = cosines(i, line[j, start * LANES:stop * LANES, :])
        for k in range(start, stop):
            at = pl.ds(k * LANES, LANES)
            keep = seen[...] == line_tag[j, k:k + 1, :]
            cut = cos[:, (k - start) * LANES:(k - start + 1) * LANES]
            part = jnp.where(keep, cut, -1.0)
            line_out[j, :, at] = jnp.maximum(
                line_out[j, :, at], jnp.max(part, axis=0, keepdims=True)
            )
            reached[...] = jnp.maximum(reached[...], part)

    def back_copy(i):
        return pltpu.make_async_remote_copy(
            src_ref=plane_out.at[i], dst_ref=plane_in.at[i],
            send_sem=back_send.at[i], recv_sem=back_recv.at[i],
            device_id=member(i), device_id_type=MESH,
        )

    def home_copy(j):
        return pltpu.make_async_remote_copy(
            src_ref=line_out.at[j], dst_ref=line_in.at[j],
            send_sem=home_send.at[j], recv_sem=home_recv.at[j],
            device_id=(lax.rem(g + steps[j], groups), m), device_id_type=MESH,
        )

    def across_lines(i, p):
        see(i)
        reached[...] = jnp.full((rows, LANES), -1.0, jnp.float32)
        for j in range(lines):
            if_takes(j, lambda j=j: line_pairs(j, i, p))
        best = jnp.max(jnp.transpose(reached[...]), axis=0, keepdims=True)
        plane_out[i] = jnp.maximum(plane_out[i], best)

    for p in range(2):
        for j in range(lines):
            if_takes(j, lambda j=j, p=p: line_copy(j, p).wait_recv())

        def step(i, carry, p=p):
            across_lines(i, p)
            if p == 1:
                back_copy(i).start()
            return carry

        lax.fori_loop(1, members, step, 0)
        across_lines(0, p)

    for j in range(lines):
        if_takes(j, lambda j=j: home_copy(j).start())

    own_best[...] = jnp.maximum(own_best[...], plane_out[0])

    def collect(i, carry):
        back_copy(i).wait_recv()
        own_best[...] = jnp.maximum(own_best[...], plane_in[i])
        return carry

    lax.fori_loop(1, members, collect, 0)

    def collect_home(j):
        home_copy(j).wait_recv()
        own_best[...] = jnp.maximum(own_best[...], line_in[j])

    for j in range(lines):
        if_gives(j, lambda j=j: collect_home(j))
    out_ref[...] = own_best[0:1, :]

    for j in range(lines):
        for p in range(2):
            if_gives(j, lambda j=j, p=p: line_copy(j, p).wait_send())
        if_gives(j, lambda j=j: end_copy(j).wait_send())
        if_takes(j, lambda j=j: home_copy(j).wait_send())
    for h in range(2):
        for slot in range(2, members, 2):
            plane_copy(*plan[slot, h], h).wait_send()
        for slot in range(0, members, 2):
            plane_copy(slot, 1, h).wait_send()
    for i in range(1, members):
        tag_copy(i).wait_send()
        back_copy(i).wait_send()


def per_device(embeddings, row_target):
    rows, width = embeddings.shape
    groups = lax.axis_size("grp")
    members = lax.axis_size("mem")
    lines = groups // 2
    dma = pltpu.SemaphoreType.DMA
    f32 = jnp.float32
    best = pl.pallas_call(
        functools.partial(kernel, groups, members),
        out_shape=jax.ShapeDtypeStruct((1, rows), f32),
        in_specs=[pl.BlockSpec(memory_space=pltpu.VMEM)] * 2,
        out_specs=pl.BlockSpec(memory_space=pltpu.VMEM),
        scratch_shapes=[
            pltpu.VMEM((members, rows, width), jnp.bfloat16),
            pltpu.VMEM((lines, rows, width), jnp.bfloat16),
            pltpu.VMEM((members, SUBLANES, LANES), f32),
            pltpu.VMEM((lines, SUBLANES, LANES), f32),
            pltpu.VMEM((rows, LANES), f32),
            pltpu.VMEM((rows, LANES), f32),
            pltpu.VMEM((members, SUBLANES, rows), f32),
            pltpu.VMEM((lines, SUBLANES, rows), f32),
            pltpu.VMEM((members, SUBLANES, rows), f32),
            pltpu.VMEM((lines, SUBLANES, rows), f32),
            pltpu.VMEM((SUBLANES, rows), f32),
            dma((members, 2)),
            dma((members, 2)),
            dma((lines, 2)),
            dma((lines, 2)),
            dma((members,)),
            dma((members,)),
            dma((lines,)),
            dma((lines,)),
            dma((members,)),
            dma((members,)),
            dma((lines,)),
            dma((lines,)),
        ],
        compiler_params=pltpu.CompilerParams(
            collective_id=0, has_side_effects=True, vmem_limit_bytes=48 * 2**20
        ),
    )(embeddings, row_target.reshape(1, rows))
    return best.reshape(rows)


def solution(mesh):
    in_specs = (P(("grp", "mem"), None), P(("grp", "mem"), None))
    return jax.shard_map(
        per_device, mesh=mesh, in_specs=in_specs, out_specs=P(("grp", "mem")), check_vma=False
    )
```

```python
import functools
import math

import jax
import jax.numpy as jnp
from jax import lax
from jax.experimental import pallas as pl
from jax.experimental.pallas import tpu as pltpu
from jax.sharding import PartitionSpec as P

MESH = pl.DeviceIdType.MESH
LANES = 128
SUBLANES = 8


def xor(a, b, count):
    total, bit = 0, 1
    while bit < count:
        one, other = lax.rem(a // bit, 2), (b // bit) % 2
        total = total + bit * (one + other - 2 * one * other)
        bit *= 2
    return total


def kernel(
    groups, members, emb_ref, target_ref, out_ref,
    plane, line, plane_tag, line_tag, seen, reached, plane_out, line_out, plane_in, line_in, own_best,
    ring_send, ring_recv, line_send, line_recv,
    tag_send, tag_recv, end_send, end_recv,
    back_send, back_recv, home_send, home_recv,
):
    rows, width = emb_ref.shape
    pieces = rows // LANES
    g, m = lax.axis_index("grp"), lax.axis_index("mem")
    full = (groups - 1) // 2
    has_half = groups % 2 == 0
    steps = list(range(1, full + 1)) + ([groups // 2] if has_half else [])
    lines = len(steps)
    halves = [pl.ds(0, rows // 2), pl.ds(rows // 2, rows // 2)]
    parts = [(0, pieces - 1), (pieces - 1, pieces)]
    relayed = members == 8

    if has_half:
        low = lax.rem(g, groups // 2)
        upper = g // (groups // 2)
        takes_half = lax.rem(low + upper, 2) == 1
        gives_half = lax.rem(low + upper, 2) == 0

    def if_takes(j, body):
        if j < full:
            body()
        else:
            pl.when(takes_half)(body)

    def if_gives(j, body):
        if j < full:
            body()
        else:
            pl.when(gives_half)(body)

    def member(i):
        return (g, xor(m, i, members))

    def group_below(j):
        return (lax.rem(g + groups - steps[j], groups), m)

    barrier = pltpu.get_barrier_semaphore()
    for i in range(1, members):
        pl.semaphore_signal(barrier, inc=1, device_id=member(i), device_id_type=MESH)
    for i in range(1, groups):
        pl.semaphore_signal(
            barrier, inc=1, device_id=(lax.rem(g + i, groups), m), device_id_type=MESH
        )

    values = emb_ref[...].astype(jnp.float32)
    inv_norm = lax.rsqrt(jnp.mean(values * values, axis=1, keepdims=True) + 1e-06) * (
        1.0 / math.sqrt(width)
    )
    plane[0] = (values * inv_norm).astype(jnp.bfloat16)
    cluster = jnp.floor((target_ref[...].astype(jnp.float32) + 0.5) * (1.0 / members))
    plane_tag[0] = jnp.zeros((SUBLANES, LANES), jnp.float32)
    for k in range(pieces):
        plane_tag[0, k:k + 1, :] = cluster[:, k * LANES:(k + 1) * LANES]

    pl.semaphore_wait(barrier, members - 1 + groups - 1)

    def size(p):
        return (parts[p][1] - parts[p][0]) * LANES

    def base(p, j):
        return p * lines * size(0) + j * size(p)

    def line_copy(j, p):
        at = pl.ds(parts[p][0] * LANES, (parts[p][1] - parts[p][0]) * LANES)
        return pltpu.make_async_remote_copy(
            src_ref=plane.at[0, at], dst_ref=line.at[pl.ds(base(p, j), size(p))],
            send_sem=line_send.at[j, p], recv_sem=line_recv.at[j, p],
            device_id=group_below(j), device_id_type=MESH,
        )

    def plane_copy(held, to, h):
        slot = held ^ to
        return pltpu.make_async_remote_copy(
            src_ref=plane.at[held, halves[h]], dst_ref=plane.at[slot, halves[h]],
            send_sem=ring_send.at[slot, h], recv_sem=ring_recv.at[slot, h],
            device_id=member(to), device_id_type=MESH,
        )

    def tag_copy(i):
        return pltpu.make_async_remote_copy(
            src_ref=plane_tag.at[0], dst_ref=plane_tag.at[i],
            send_sem=tag_send.at[i], recv_sem=tag_recv.at[i],
            device_id=member(i), device_id_type=MESH,
        )

    def end_copy(j):
        return pltpu.make_async_remote_copy(
            src_ref=plane_tag.at[0], dst_ref=line_tag.at[j],
            send_sem=end_send.at[j], recv_sem=end_recv.at[j],
            device_id=group_below(j), device_id_type=MESH,
        )

    plan = {}
    for slot in range(2, members, 2):
        for h in range(2):
            plan[slot, h] = (0, slot)
    if relayed:
        order = [(2, 0), (4, 1), (2, 1), (4, 0), (6, 0), (6, 1)]
        plan[6, 0], plan[6, 1] = (2, 4), (4, 2)
    else:
        order = [(slot, h) for slot in range(2, members, 2) for h in range(2)]

    for i in range(1, members):
        tag_copy(i).start()
    for j in range(lines):
        if_gives(j, lambda j=j: end_copy(j).start())
    first = [key for key in order if plan[key][0] == 0]
    for p in range(2):
        for h, to in [(h, to) for to, h in first[p * len(first) // 2:(p + 1) * len(first) // 2]]:
            plane_copy(0, to, h).start()
        for j in range(lines):
            if_gives(j, lambda j=j, p=p: line_copy(j, p).start())
    for h in range(2):
        plane_copy(0, 1, h).start()

    def see(i):
        for k in range(pieces):
            row = jnp.broadcast_to(plane_tag[i, k:k + 1, :], (LANES, LANES))
            seen[i, k * LANES:(k + 1) * LANES, :] = jnp.transpose(row)

    def cosines(i, left):
        return lax.dot_general(
            plane[i], left, (((1,), (1,)), ((), ())), preferred_element_type=jnp.float32
        )

    own_best[...] = jnp.full((SUBLANES, rows), -1.0, jnp.float32)
    line_out[...] = jnp.full((lines, SUBLANES, rows), -1.0, jnp.float32)
    plane_out[...] = jnp.full((members, SUBLANES, rows), -1.0, jnp.float32)

    def own_pairs(i, same=False):
        cos = cosines(i, plane[0])
        for k in range(pieces):
            at = pl.ds(k * LANES, LANES)
            keep = seen[i] == plane_tag[0, k:k + 1, :]
            if same:
                down = lax.broadcasted_iota(jnp.int32, (rows, LANES), 0)
                over = lax.broadcasted_iota(jnp.int32, (rows, LANES), 1) + k * LANES
                keep = keep & (down != over)
            part = jnp.where(keep, cos[:, k * LANES:(k + 1) * LANES], -1.0)
            own_best[:, at] = jnp.maximum(own_best[:, at], jnp.max(part, axis=0, keepdims=True))

    see(0)
    own_pairs(0, True)
    for i in range(1, members):
        tag_copy(i).wait_recv()
        see(i)
    for j in range(lines):
        if_takes(j, lambda j=j: end_copy(j).wait_recv())

    def arrive(slot, h):
        held, to = plan[slot, h]
        plane_copy(held, to, h).wait_recv()
        for key, (source, onto) in plan.items():
            if source == slot and key[1] == h:
                plane_copy(source, onto, h).start()
        plane_copy(slot, 1, h).start()

    def line_pairs(i, p, count):
        if count == 0:
            return
        start, stop = parts[p]
        cos = cosines(i, line[base(p, 0):base(p, count), :])
        best = None
        for j in range(count):
            for k in range(start, stop):
                at = pl.ds(k * LANES, LANES)
                c = j * (stop - start) + k - start
                keep = seen[i] == line_tag[j, k:k + 1, :]
                part = jnp.where(keep, cos[:, c * LANES:(c + 1) * LANES], -1.0)
                line_out[j, :, at] = jnp.maximum(
                    line_out[j, :, at], jnp.max(part, axis=0, keepdims=True)
                )
                best = part if best is None else jnp.maximum(best, part)
        if p == 0:
            reached[i] = best
        else:
            best = jnp.transpose(jnp.maximum(best, reached[i]))
            plane_out[i] = jnp.broadcast_to(jnp.max(best, axis=0, keepdims=True), (SUBLANES, rows))

    def taken(body):
        if has_half:
            pl.when(takes_half)(lambda: body(lines))
            pl.when(gives_half)(lambda: body(full))
        else:
            body(lines)

    def first_parts(start, stop):
        def loop(count):
            def step(i, carry):
                line_pairs(i, 0, count)
                return carry

            lax.fori_loop(start, stop, step, 0)

        taken(loop)

    def back_copy(i):
        return pltpu.make_async_remote_copy(
            src_ref=plane_out.at[i], dst_ref=plane_in.at[i],
            send_sem=back_send.at[i], recv_sem=back_recv.at[i],
            device_id=member(i), device_id_type=MESH,
        )

    def home_copy(j):
        return pltpu.make_async_remote_copy(
            src_ref=line_out.at[j], dst_ref=line_in.at[j],
            send_sem=home_send.at[j], recv_sem=home_recv.at[j],
            device_id=(lax.rem(g + steps[j], groups), m), device_id_type=MESH,
        )

    def wait_line(p):
        for j in range(lines):
            if_takes(j, lambda j=j, p=p: line_copy(j, p).wait_recv())

    def from_partner(i):
        for h in range(2):
            plane_copy(i - 1, 1, h).wait_recv()
        own_pairs(i)

    from_partner(1)
    late = 2 if relayed else 0
    early = len(order) - late
    for slot, h in order[:early]:
        arrive(slot, h)
    reach = 2 + early
    for i in range(2, reach, 2):
        own_pairs(i)
    for i in range(3, reach, 2):
        from_partner(i)
    wait_line(0)
    first_parts(0, 2)
    for slot, h in order[early:]:
        arrive(slot, h)
    first_parts(2, reach)
    if late:
        own_pairs(reach)
        first_parts(reach, reach + 1)
        from_partner(reach + 1)
        first_parts(reach + 1, reach + 2)
    wait_line(1)

    def last_parts(count):
        line_pairs(0, 1, count)
        line_pairs(1, 1, count)
        back_copy(1).start()

        def step(t, carry):
            line_pairs(2 * t, 1, count)
            line_pairs(2 * t + 1, 1, count)
            back_copy(2 * t).start()
            back_copy(2 * t + 1).start()
            return carry

        lax.fori_loop(1, members // 2, step, 0)

    taken(last_parts)

    for j in range(lines):
        if_takes(j, lambda j=j: home_copy(j).start())

    own_best[...] = jnp.maximum(own_best[...], plane_out[0])

    def collect(i, carry):
        back_copy(i).wait_recv()
        own_best[...] = jnp.maximum(own_best[...], plane_in[i])
        return carry

    lax.fori_loop(1, members, collect, 0)

    def collect_home(j):
        home_copy(j).wait_recv()
        own_best[...] = jnp.maximum(own_best[...], line_in[j])

    for j in range(lines):
        if_gives(j, lambda j=j: collect_home(j))
    out_ref[...] = own_best[0:1, :]

    for j in range(lines):
        for p in range(2):
            if_gives(j, lambda j=j, p=p: line_copy(j, p).wait_send())
        if_gives(j, lambda j=j: end_copy(j).wait_send())
        if_takes(j, lambda j=j: home_copy(j).wait_send())
    for h in range(2):
        for slot in range(2, members, 2):
            plane_copy(*plan[slot, h], h).wait_send()
        for slot in range(0, members, 2):
            plane_copy(slot, 1, h).wait_send()
    for i in range(1, members):
        tag_copy(i).wait_send()
        back_copy(i).wait_send()


def per_device(embeddings, row_target):
    rows, width = embeddings.shape
    groups = lax.axis_size("grp")
    members = lax.axis_size("mem")
    lines = groups // 2
    dma = pltpu.SemaphoreType.DMA
    f32 = jnp.float32
    best = pl.pallas_call(
        functools.partial(kernel, groups, members),
        out_shape=jax.ShapeDtypeStruct((1, rows), f32),
        in_specs=[pl.BlockSpec(memory_space=pltpu.VMEM)] * 2,
        out_specs=pl.BlockSpec(memory_space=pltpu.VMEM),
        scratch_shapes=[
            pltpu.VMEM((members, rows, width), jnp.bfloat16),
            pltpu.VMEM((lines * rows, width), jnp.bfloat16),
            pltpu.VMEM((members, SUBLANES, LANES), f32),
            pltpu.VMEM((lines, SUBLANES, LANES), f32),
            pltpu.VMEM((members, rows, LANES), f32),
            pltpu.VMEM((members, rows, LANES), f32),
            pltpu.VMEM((members, SUBLANES, rows), f32),
            pltpu.VMEM((lines, SUBLANES, rows), f32),
            pltpu.VMEM((members, SUBLANES, rows), f32),
            pltpu.VMEM((lines, SUBLANES, rows), f32),
            pltpu.VMEM((SUBLANES, rows), f32),
            dma((members, 2)),
            dma((members, 2)),
            dma((lines, 2)),
            dma((lines, 2)),
            dma((members,)),
            dma((members,)),
            dma((lines,)),
            dma((lines,)),
            dma((members,)),
            dma((members,)),
            dma((lines,)),
            dma((lines,)),
        ],
        compiler_params=pltpu.CompilerParams(
            collective_id=0, has_side_effects=True, vmem_limit_bytes=48 * 2**20
        ),
    )(embeddings, row_target.reshape(1, rows))
    return best.reshape(rows)


def solution(mesh):
    in_specs = (P(("grp", "mem"), None), P(("grp", "mem"), None))
    return jax.shard_map(
        per_device, mesh=mesh, in_specs=in_specs, out_specs=P(("grp", "mem")), check_vma=False
    )
```

```python
import functools
import math

import jax
import jax.numpy as jnp
from jax import lax
from jax.experimental import pallas as pl
from jax.experimental.pallas import tpu as pltpu
from jax.sharding import PartitionSpec as P

MESH = pl.DeviceIdType.MESH
LANES = 128
SUBLANES = 8


def xor(a, b, count):
    total, bit = 0, 1
    while bit < count:
        one, other = lax.rem(a // bit, 2), (b // bit) % 2
        total = total + bit * (one + other - 2 * one * other)
        bit *= 2
    return total


def kernel(
    groups, members, emb_ref, target_ref, out_ref,
    plane, line, plane_tag, line_tag, seen, reached, plane_out, line_out, plane_in, line_in, own_best,
    ring_send, ring_recv, line_send, line_recv,
    tag_send, tag_recv, end_send, end_recv,
    back_send, back_recv, home_send, home_recv,
):
    rows, width = emb_ref.shape
    pieces = rows // LANES
    g, m = lax.axis_index("grp"), lax.axis_index("mem")
    full = (groups - 1) // 2
    has_half = groups % 2 == 0
    steps = list(range(1, full + 1)) + ([groups // 2] if has_half else [])
    lines = len(steps)
    halves = [pl.ds(0, rows // 2), pl.ds(rows // 2, rows // 2)]
    parts = [(0, pieces - 1), (pieces - 1, pieces)]
    relayed = members == 8

    if has_half:
        low = lax.rem(g, groups // 2)
        upper = g // (groups // 2)
        takes_half = lax.rem(low + upper, 2) == 1
        gives_half = lax.rem(low + upper, 2) == 0

    def if_takes(j, body):
        if j < full:
            body()
        else:
            pl.when(takes_half)(body)

    def if_gives(j, body):
        if j < full:
            body()
        else:
            pl.when(gives_half)(body)

    def member(i):
        return (g, xor(m, i, members))

    def group_below(j):
        return (lax.rem(g + groups - steps[j], groups), m)

    barrier = pltpu.get_barrier_semaphore()
    for i in range(1, members):
        pl.semaphore_signal(barrier, inc=1, device_id=member(i), device_id_type=MESH)
    for i in range(1, groups):
        pl.semaphore_signal(
            barrier, inc=1, device_id=(lax.rem(g + i, groups), m), device_id_type=MESH
        )

    def normalize(start, stop):
        values = emb_ref[start:stop, :].astype(jnp.float32)
        inv_norm = lax.rsqrt(jnp.mean(values * values, axis=1, keepdims=True) + 1e-06) * (
            1.0 / math.sqrt(width)
        )
        plane[0, start:stop, :] = (values * inv_norm).astype(jnp.bfloat16)

    cut = parts[0][1] * LANES
    normalize(0, cut)
    cluster = jnp.floor((target_ref[...].astype(jnp.float32) + 0.5) * (1.0 / members))
    plane_tag[0] = jnp.zeros((SUBLANES, LANES), jnp.float32)
    for k in range(pieces):
        plane_tag[0, k:k + 1, :] = cluster[:, k * LANES:(k + 1) * LANES]

    pl.semaphore_wait(barrier, members - 1 + groups - 1)

    def size(p):
        return (parts[p][1] - parts[p][0]) * LANES

    def base(p, j):
        return p * lines * size(0) + j * size(p)

    def line_copy(j, p):
        at = pl.ds(parts[p][0] * LANES, (parts[p][1] - parts[p][0]) * LANES)
        return pltpu.make_async_remote_copy(
            src_ref=plane.at[0, at], dst_ref=line.at[pl.ds(base(p, j), size(p))],
            send_sem=line_send.at[j, p], recv_sem=line_recv.at[j, p],
            device_id=group_below(j), device_id_type=MESH,
        )

    def plane_copy(held, to, h):
        slot = held ^ to
        return pltpu.make_async_remote_copy(
            src_ref=plane.at[held, halves[h]], dst_ref=plane.at[slot, halves[h]],
            send_sem=ring_send.at[slot, h], recv_sem=ring_recv.at[slot, h],
            device_id=member(to), device_id_type=MESH,
        )

    def tag_copy(i):
        return pltpu.make_async_remote_copy(
            src_ref=plane_tag.at[0], dst_ref=plane_tag.at[i],
            send_sem=tag_send.at[i], recv_sem=tag_recv.at[i],
            device_id=member(i), device_id_type=MESH,
        )

    def end_copy(j):
        return pltpu.make_async_remote_copy(
            src_ref=plane_tag.at[0], dst_ref=line_tag.at[j],
            send_sem=end_send.at[j], recv_sem=end_recv.at[j],
            device_id=group_below(j), device_id_type=MESH,
        )

    plan = {}
    for slot in range(2, members, 2):
        for h in range(2):
            plan[slot, h] = (0, slot)
    if relayed:
        order = [(2, 0), (4, 1), (2, 1), (4, 0), (6, 0), (6, 1)]
        plan[6, 0], plan[6, 1] = (2, 4), (4, 2)
    else:
        order = [(slot, h) for slot in range(2, members, 2) for h in range(2)]

    first = [key for key in order if plan[key][0] == 0]
    for j in range(lines):
        if_gives(j, lambda j=j: line_copy(j, 0).start())
    for slot, h in first:
        if h == 0:
            plane_copy(0, slot, h).start()
    normalize(cut, rows)
    for slot, h in first:
        if h == 1:
            plane_copy(0, slot, h).start()
    for j in range(lines):
        if_gives(j, lambda j=j: line_copy(j, 1).start())
    for i in range(1, members):
        tag_copy(i).start()
    for j in range(lines):
        if_gives(j, lambda j=j: end_copy(j).start())
    for h in range(2):
        plane_copy(0, 1, h).start()

    def see(i):
        for k in range(pieces):
            row = jnp.broadcast_to(plane_tag[i, k:k + 1, :], (LANES, LANES))
            seen[i, k * LANES:(k + 1) * LANES, :] = jnp.transpose(row)

    def cosines(i, left):
        return lax.dot_general(
            plane[i], left, (((1,), (1,)), ((), ())), preferred_element_type=jnp.float32
        )

    own_best[...] = jnp.full((SUBLANES, rows), -1.0, jnp.float32)
    line_out[...] = jnp.full((lines, SUBLANES, rows), -1.0, jnp.float32)
    plane_out[...] = jnp.full((members, SUBLANES, rows), -1.0, jnp.float32)

    def own_pairs(i, same=False):
        cos = cosines(i, plane[0])
        for k in range(pieces):
            at = pl.ds(k * LANES, LANES)
            keep = seen[i] == plane_tag[0, k:k + 1, :]
            if same:
                down = lax.broadcasted_iota(jnp.int32, (rows, LANES), 0)
                over = lax.broadcasted_iota(jnp.int32, (rows, LANES), 1) + k * LANES
                keep = keep & (down != over)
            part = jnp.where(keep, cos[:, k * LANES:(k + 1) * LANES], -1.0)
            own_best[:, at] = jnp.maximum(own_best[:, at], jnp.max(part, axis=0, keepdims=True))

    see(0)
    own_pairs(0, True)
    for i in range(1, members):
        tag_copy(i).wait_recv()
        see(i)
    for j in range(lines):
        if_takes(j, lambda j=j: end_copy(j).wait_recv())

    def arrive(slot, h):
        held, to = plan[slot, h]
        plane_copy(held, to, h).wait_recv()
        for key, (source, onto) in plan.items():
            if source == slot and key[1] == h:
                plane_copy(source, onto, h).start()
        plane_copy(slot, 1, h).start()

    def line_pairs(i, p, count):
        if count == 0:
            return
        start, stop = parts[p]
        cos = cosines(i, line[base(p, 0):base(p, count), :])
        best = None
        for j in range(count):
            for k in range(start, stop):
                at = pl.ds(k * LANES, LANES)
                c = j * (stop - start) + k - start
                keep = seen[i] == line_tag[j, k:k + 1, :]
                part = jnp.where(keep, cos[:, c * LANES:(c + 1) * LANES], -1.0)
                line_out[j, :, at] = jnp.maximum(
                    line_out[j, :, at], jnp.max(part, axis=0, keepdims=True)
                )
                best = part if best is None else jnp.maximum(best, part)
        if p == 0:
            reached[i] = best
        else:
            best = jnp.transpose(jnp.maximum(best, reached[i]))
            plane_out[i] = jnp.broadcast_to(jnp.max(best, axis=0, keepdims=True), (SUBLANES, rows))

    def taken(body):
        if has_half:
            pl.when(takes_half)(lambda: body(lines))
            pl.when(gives_half)(lambda: body(full))
        else:
            body(lines)

    def first_parts(start, stop):
        def loop(count):
            def step(i, carry):
                line_pairs(i, 0, count)
                return carry

            lax.fori_loop(start, stop, step, 0)

        taken(loop)

    def back_copy(i):
        return pltpu.make_async_remote_copy(
            src_ref=plane_out.at[i], dst_ref=plane_in.at[i],
            send_sem=back_send.at[i], recv_sem=back_recv.at[i],
            device_id=member(i), device_id_type=MESH,
        )

    def home_copy(j):
        return pltpu.make_async_remote_copy(
            src_ref=line_out.at[j], dst_ref=line_in.at[j],
            send_sem=home_send.at[j], recv_sem=home_recv.at[j],
            device_id=(lax.rem(g + steps[j], groups), m), device_id_type=MESH,
        )

    def wait_line(p):
        for j in range(lines):
            if_takes(j, lambda j=j, p=p: line_copy(j, p).wait_recv())

    def from_partner(i):
        for h in range(2):
            plane_copy(i - 1, 1, h).wait_recv()
        own_pairs(i)

    from_partner(1)
    late = 2 if relayed else 0
    early = len(order) - late
    for slot, h in order[:early]:
        arrive(slot, h)
    reach = 2 + early
    for i in range(2, reach, 2):
        own_pairs(i)
    for i in range(3, reach, 2):
        from_partner(i)
    wait_line(0)
    first_parts(0, 2)
    for slot, h in order[early:]:
        arrive(slot, h)
    first_parts(2, reach)
    if late:
        own_pairs(reach)
        first_parts(reach, reach + 1)
        from_partner(reach + 1)
        first_parts(reach + 1, reach + 2)
    wait_line(1)

    def last_parts(count):
        line_pairs(0, 1, count)
        line_pairs(1, 1, count)
        back_copy(1).start()

        def step(t, carry):
            line_pairs(2 * t, 1, count)
            line_pairs(2 * t + 1, 1, count)
            back_copy(2 * t).start()
            back_copy(2 * t + 1).start()
            return carry

        lax.fori_loop(1, members // 2, step, 0)

    taken(last_parts)

    for j in range(lines):
        if_takes(j, lambda j=j: home_copy(j).start())

    own_best[...] = jnp.maximum(own_best[...], plane_out[0])

    def collect(i, carry):
        back_copy(i).wait_recv()
        own_best[...] = jnp.maximum(own_best[...], plane_in[i])
        return carry

    lax.fori_loop(1, members, collect, 0)

    def collect_home(j):
        home_copy(j).wait_recv()
        own_best[...] = jnp.maximum(own_best[...], line_in[j])

    for j in range(lines):
        if_gives(j, lambda j=j: collect_home(j))
    out_ref[...] = own_best[0:1, :]

    for j in range(lines):
        for p in range(2):
            if_gives(j, lambda j=j, p=p: line_copy(j, p).wait_send())
        if_gives(j, lambda j=j: end_copy(j).wait_send())
        if_takes(j, lambda j=j: home_copy(j).wait_send())
    for h in range(2):
        for slot in range(2, members, 2):
            plane_copy(*plan[slot, h], h).wait_send()
        for slot in range(0, members, 2):
            plane_copy(slot, 1, h).wait_send()
    for i in range(1, members):
        tag_copy(i).wait_send()
        back_copy(i).wait_send()


def per_device(embeddings, row_target):
    rows, width = embeddings.shape
    groups = lax.axis_size("grp")
    members = lax.axis_size("mem")
    lines = groups // 2
    dma = pltpu.SemaphoreType.DMA
    f32 = jnp.float32
    best = pl.pallas_call(
        functools.partial(kernel, groups, members),
        out_shape=jax.ShapeDtypeStruct((1, rows), f32),
        in_specs=[pl.BlockSpec(memory_space=pltpu.VMEM)] * 2,
        out_specs=pl.BlockSpec(memory_space=pltpu.VMEM),
        scratch_shapes=[
            pltpu.VMEM((members, rows, width), jnp.bfloat16),
            pltpu.VMEM((lines * rows, width), jnp.bfloat16),
            pltpu.VMEM((members, SUBLANES, LANES), f32),
            pltpu.VMEM((lines, SUBLANES, LANES), f32),
            pltpu.VMEM((members, rows, LANES), f32),
            pltpu.VMEM((members, rows, LANES), f32),
            pltpu.VMEM((members, SUBLANES, rows), f32),
            pltpu.VMEM((lines, SUBLANES, rows), f32),
            pltpu.VMEM((members, SUBLANES, rows), f32),
            pltpu.VMEM((lines, SUBLANES, rows), f32),
            pltpu.VMEM((SUBLANES, rows), f32),
            dma((members, 2)),
            dma((members, 2)),
            dma((lines, 2)),
            dma((lines, 2)),
            dma((members,)),
            dma((members,)),
            dma((lines,)),
            dma((lines,)),
            dma((members,)),
            dma((members,)),
            dma((lines,)),
            dma((lines,)),
        ],
        compiler_params=pltpu.CompilerParams(
            collective_id=0, has_side_effects=True, vmem_limit_bytes=48 * 2**20
        ),
    )(embeddings, row_target.reshape(1, rows))
    return best.reshape(rows)


def solution(mesh):
    in_specs = (P(("grp", "mem"), None), P(("grp", "mem"), None))
    return jax.shard_map(
        per_device, mesh=mesh, in_specs=in_specs, out_specs=P(("grp", "mem")), check_vma=False
    )
```
